256 devices in a mesh: line: 128 (over x, y, z), tm: 2 (over core).
Axes of the slice: x: 4, y: 4, z: 8, core: 2. Of those that a mesh axis runs over, the one named last changes fastest.
Arguments:
- signal: bfloat16 [4096, 8192], P('line', 'tm'), may hold values from -6 to 6
- cotangent: bfloat16 [4096, 8192], P('line', 'tm'), may hold values from -6 to 6
- bank: bfloat16 [16384, 512], P('line'), may hold values from -0.5 to 0.5
- lengths: int32 [4096], P('line'), may hold values from 1 to 512
- kernel_ids: int32 [4096], P('line'), may hold values from 0 to 16383, as said below
Outputs:
- filtered: bfloat16 [4096, 8192], P('line', 'tm')
- signal_grad: bfloat16 [4096, 8192], P('line', 'tm')
- bank_grad: float32 [16384, 512], P('line', 'tm')
The draws below stay inside these ranges and needn't reach their ends.
Inputs may be any that keep to these rules, and one draw needn't show every extreme that they name: `kernel_ids`: row k of the bank is held by the device of index k // 128 along line. Among the 32 lines of one device, at most 2 use rows held by one owner, and some owner's rows are used by exactly 2 lines of every device.
All inputs are finite; a program needn't handle non-finite values.
Results may differ from the reference program's by a relative error of at most 0.0075.
Values may be sent and summed in bfloat16 or wider, within the bound.
A program may use at most 128 MiB of HBM per device.

```python
import math
import jax
import jax.numpy as jnp
from jax import lax

LINES_DEV = 32
TAPS = 512
KSLOT = 128
CAP = 2
LINES = 4096
TIME = 8192
KERNELS = 16384


def draw_lengths(key, part):
    block_total = LINES // LINES_DEV
    quarter = TAPS // 4
    key_caps, key_force, key_lens, key_spot = jax.random.split(key, 4)
    levels = jax.random.randint(key_caps, (block_total,), 1, 5) * quarter
    forced = jax.random.randint(key_force, (), 0, block_total)
    levels = jnp.where(jnp.arange(block_total) == forced, TAPS, levels)
    drawn = jax.random.randint(key_lens, (block_total, LINES_DEV), 1, levels[:, None] + 1)
    spots = jax.random.randint(key_spot, (block_total,), 0, LINES_DEV)
    drawn = jnp.where(jnp.arange(LINES_DEV)[None, :] == spots[:, None], levels[:, None], drawn)
    return drawn.reshape(LINES).astype(jnp.int32)


def draw_kernel_ids(key, part):
    block_total = LINES // LINES_DEV
    owner_total = KERNELS // KSLOT
    group_total = LINES_DEV // CAP
    key_star, key_order, key_shuffle, key_slots = jax.random.split(key, 4)
    central = jax.random.randint(key_star, (), 0, owner_total)
    orders = jax.vmap(lambda k: jax.random.permutation(k, owner_total))(jax.random.split(key_order, block_total))
    firsts = orders[:, :1]
    orders = jnp.where(orders == central, firsts, orders)
    orders = jnp.where(jnp.arange(owner_total)[None, :] == 0, central, orders)
    holders = jnp.repeat(orders[:, :group_total], CAP, axis=1)
    shuffle = jax.vmap(lambda k: jax.random.permutation(k, LINES_DEV))(jax.random.split(key_shuffle, block_total))
    holders = jnp.take_along_axis(holders, shuffle, axis=1)
    slots_drawn = jax.random.randint(key_slots, (block_total, LINES_DEV), 0, KSLOT)
    return (holders * KSLOT + slots_drawn).reshape(LINES).astype(jnp.int32)


def shard_levels(key, dims, pieces, low, high):
    factor_of = 1.0
    for dim, parts in pieces:
        steps = jax.random.uniform(jax.random.fold_in(jax.random.fold_in(key, 6), dim), (parts,), jnp.float32, low / len(pieces), high / len(pieces))
        factor_of = factor_of * jnp.repeat(jnp.exp(steps), dims[dim] // parts).reshape((-1,) + (1,) * (len(dims) - 1 - dim))
    return factor_of


def scatter_about(stream_key, shape, scale, limit, cuts=(), kind=jnp.bfloat16):
    values = jax.random.normal(stream_key, shape, jnp.float32) * scale
    if len(cuts) > 0:
        values = shard_levels(stream_key, shape, cuts, -0.22, 0.18) * values
    return jnp.clip(values, min=-limit, max=limit).astype(kind)


def setup_inputs(seed: int = 0) -> dict:
    keys = jax.random.split(jax.random.key(seed), 6)
    signal = scatter_about(keys[0], (LINES, TIME), 1.0, 6.0, ((0, 128), (1, 2)))
    cotangent = scatter_about(keys[1], (LINES, TIME), 1.0, 6.0, ((0, 128), (1, 2)))
    bank = scatter_about(keys[2], (KERNELS, TAPS), (TAPS // 4) ** -0.5, 0.5, ((0, 128),))
    lengths = draw_lengths(jax.random.fold_in(keys[5], 71), 0)
    kernel_ids = draw_kernel_ids(jax.random.fold_in(keys[5], 71), 0)
    return {"signal": signal, "cotangent": cotangent, "bank": bank, "lengths": lengths, "kernel_ids": kernel_ids}


def reference(signal, cotangent, bank, lengths, kernel_ids):
    tap_mask = jnp.arange(TAPS)[None, :] < lengths[:, None]
    kernels = jnp.where(tap_mask, bank[kernel_ids].astype(jnp.float32), jnp.float32(0.0))
    fft_len = 2 * TIME
    block_total = LINES // LINES_DEV

    def filter_block(group_item):
        signal_rows, cotan_rows, kernel_rows = group_item
        signal_rows = signal_rows.astype(jnp.float32)
        cotan_rows = cotan_rows.astype(jnp.float32)
        signal_freq = jnp.fft.rfft(signal_rows, n=fft_len, axis=1)
        cotan_freq = jnp.fft.rfft(cotan_rows, n=fft_len, axis=1)
        kernel_freq = jnp.fft.rfft(kernel_rows, n=fft_len, axis=1)
        forward = jnp.fft.irfft(signal_freq * kernel_freq, n=fft_len, axis=1)[:, :TIME]
        backward = jnp.fft.irfft(cotan_freq * jnp.conj(kernel_freq), n=fft_len, axis=1)[:, :TIME]
        lagged = jnp.fft.irfft(cotan_freq * jnp.conj(signal_freq), n=fft_len, axis=1)[:, :TAPS]
        return (forward.astype(jnp.bfloat16), backward.astype(jnp.bfloat16), lagged.astype(jnp.float32))
    forward, backward, lagged = lax.map(filter_block, (signal.reshape(block_total, LINES_DEV, TIME), cotangent.reshape(block_total, LINES_DEV, TIME), kernels.reshape(block_total, LINES_DEV, TAPS)))
    lag_grad = jnp.where(tap_mask, lagged.reshape(LINES, TAPS), jnp.float32(0.0)) * (1.0 / math.sqrt(TIME))
    bank_grad = jax.ops.segment_sum(lag_grad, kernel_ids, num_segments=KERNELS)
    return (forward.reshape(LINES, TIME), backward.reshape(LINES, TIME), bank_grad)
```

```python
import math

import jax
import jax.numpy as jnp
from jax import lax
from jax.experimental import pallas as pl
from jax.experimental.pallas import tpu as pltpu
from jax.sharding import PartitionSpec as P

MESH = pl.DeviceIdType.MESH
BF = jnp.bfloat16
F32 = jnp.float32
LINES = 32
TAPS = 512
LANES = 128
SHIFTS = TAPS // LANES
SLOTS = 2
BANK_ROWS = 128


def iota(shape, dim):
    return lax.broadcasted_iota(jnp.int32, shape, dim)


def column(row):
    size = row.shape[1]
    mask = iota((size, size), 0) == iota((size, size), 1)
    return jnp.sum(jnp.where(mask, jnp.broadcast_to(row, (size, size)), 0.0), axis=1, keepdims=True)


def one_hot(hit):
    return jnp.where(hit, 1.0, 0.0)


def kernel(
    sig_hbm, cot_hbm, bank_hbm, len_ref, ids_ref,
    fil_hbm, grad_hbm, bgrad_hbm,
    sig, cot, bank, fil, grad, bgrad,
    halo, rq_out, rq_in, fe_out, fe_in, re_out, re_in,
    kx_out, kx_in, lx_out, lx_in, gx_out, gx_in,
    xf, cf, cjf, xjf, lhs, acc, kf, stage, owned, of, gf,
    in_sem, out_sem, halo_sem, rq_sem, fe_sem, re_sem, kx_sem, lx_sem, gx_sem,
):
    me = lax.axis_index("line")
    core = lax.axis_index("tm")
    other = (me, 1 - core)
    blocks = sig.shape[1] // LANES
    chips = rq_out.shape[0]
    par = lax.rem(me + core, 2)
    place = lax.div(me, 2)
    here_z = lax.rem(place, 4)
    here_y = lax.rem(lax.div(place, 4), 4)
    here_x = lax.div(place, 16)

    ins = [
        pltpu.make_async_copy(sig_hbm, sig, in_sem.at[0]),
        pltpu.make_async_copy(cot_hbm, cot, in_sem.at[1]),
        pltpu.make_async_copy(bank_hbm, bank, in_sem.at[2]),
    ]
    for copy in ins:
        copy.start()

    def peer(step):
        a = step // 16
        b = (step // 4) % 4
        c = step % 4
        z = lax.rem(here_z + 2 + (a * (a + 1)) // 2, 4)
        x = lax.rem(here_x + 2 + (b * (b + 1)) // 2, 4)
        y = lax.rem(here_y + 2 + (c * (c + 1)) // 2, 4)
        return x * 16 + y * 4 + z

    barrier = pltpu.get_barrier_semaphore()

    def greet(step, carry):
        pl.semaphore_signal(
            barrier, inc=1, device_id=(2 * peer(step) + par, core), device_id_type=MESH
        )
        return carry

    lax.fori_loop(0, chips - 1, greet, 0)

    @pl.when(core == 1)
    def _():
        pl.semaphore_signal(barrier, inc=1, device_id=(2 * place + par, core), device_id_type=MESH)

    pl.semaphore_signal(barrier, inc=1, device_id=other, device_id_type=MESH)

    def scatter(out_ref, in_ref, sems):
        def send(step, carry):
            i = peer(step)
            pltpu.make_async_remote_copy(
                src_ref=out_ref.at[i],
                dst_ref=in_ref.at[place],
                send_sem=sems.at[0],
                recv_sem=sems.at[1],
                device_id=(2 * i + par, core),
                device_id_type=MESH,
            ).start()
            return carry

        lax.fori_loop(0, chips - 1, send, 0)

        @pl.when(core == 1)
        def _():
            pltpu.make_async_remote_copy(
                src_ref=out_ref.at[place],
                dst_ref=in_ref.at[place],
                send_sem=sems.at[0],
                recv_sem=sems.at[1],
                device_id=(2 * place + par, core),
                device_id_type=MESH,
            ).start()

        @pl.when(core == 0)
        def _():
            pltpu.make_async_copy(out_ref.at[place], in_ref.at[place], sems.at[1]).start()

    def arrived(in_ref, sems):
        pltpu.make_async_copy(in_ref, in_ref, sems.at[1]).wait()

    def departed(out_ref, sems):
        part = out_ref.at[pl.ds(0, chips - 1)]
        pltpu.make_async_copy(part, part, sems.at[0]).wait()

        @pl.when(core == 1)
        def _():
            pltpu.make_async_copy(out_ref.at[0], out_ref.at[0], sems.at[0]).wait()

    def swap(out_ref, in_ref, sems):
        return pltpu.make_async_remote_copy(
            src_ref=out_ref,
            dst_ref=in_ref,
            send_sem=sems.at[0],
            recv_sem=sems.at[1],
            device_id=other,
            device_id_type=MESH,
        )

    ids_row = ids_ref[...].reshape(1, LINES)
    holder_row = ids_row // BANK_ROWS
    inside_row = ids_row % BANK_ROWS
    holder_col = column(holder_row.astype(F32)).astype(jnp.int32)
    inside_col = column(inside_row.astype(F32)).astype(jnp.int32)
    len_col = column(len_ref[...].reshape(1, LINES).astype(F32)).astype(jnp.int32)
    same = jnp.broadcast_to(holder_col, (LINES, LINES)) == jnp.broadcast_to(holder_row, (LINES, LINES))
    subs = iota((LINES, LINES), 0)
    lanes = iota((LINES, LINES), 1)
    rank_col = jnp.sum(one_hot(same & (lanes < subs)), axis=1, keepdims=True).astype(jnp.int32)
    rank_row = jnp.sum(one_hot(same & (subs < lanes)), axis=0, keepdims=True).astype(jnp.int32)
    spot_col = jnp.where(holder_col % 2 == par, holder_col // 2, -chips * SLOTS)
    spot_row = jnp.where(holder_row % 2 == par, holder_row // 2, -chips * SLOTS)
    picks = SLOTS * chips
    pick = one_hot(iota((LINES, picks), 1) == spot_col + rank_col * chips).astype(BF)
    pick_t = one_hot(iota((picks, LINES), 0) == spot_row + rank_row * chips).astype(BF)
    wanted = jnp.where(
        iota((chips, LINES), 0) == spot_row, (rank_row + 1).astype(F32), 0.0
    ).astype(BF)
    rows = one_hot(iota((LINES, BANK_ROWS), 1) == inside_col).astype(BF)
    asks = jnp.dot(wanted, rows, preferred_element_type=F32)
    rq_out[...] = asks.reshape(chips, 1, BANK_ROWS)
    tap_mask = iota((LINES, TAPS), 1) < len_col

    for copy in ins[:2]:
        copy.wait()
    pl.semaphore_wait(barrier, chips + core)

    scatter(rq_out, rq_in, rq_sem)

    @pl.when(core == 0)
    def _():
        swap(sig.at[:, pl.ds(blocks * LANES - TAPS, TAPS)], halo, halo_sem).start()

    @pl.when(core == 1)
    def _():
        swap(cot.at[:, pl.ds(0, TAPS)], halo, halo_sem).start()

    for q in range(blocks):
        span = slice(q * LANES, (q + 1) * LANES)
        xf[(SHIFTS + q) * LINES : (SHIFTS + q + 1) * LINES, :] = sig[:, span].astype(F32)
        cf[q * LINES : (q + 1) * LINES, :] = cot[:, span].astype(F32)
    pltpu.make_async_copy(halo, halo, halo_sem.at[1]).wait()
    for s in range(SHIFTS):
        edge = halo[:, s * LANES : (s + 1) * LANES].astype(F32)
        xf[s * LINES : (s + 1) * LINES, :] = jnp.where(core == 1, edge, 0.0)
        cf[(blocks + s) * LINES : (blocks + s + 1) * LINES, :] = jnp.where(core == 0, edge, 0.0)
    turn = one_hot(iota((LANES, LANES), 0) + iota((LANES, LANES), 1) == LANES - 1).astype(BF)
    flip_rows = 4 * LINES

    def flip(step, carry):
        at = pl.ds(pl.multiple_of(step * flip_rows, flip_rows), flip_rows)
        cjf[at, :] = jnp.dot(cf[at, :].astype(BF), turn, preferred_element_type=F32)
        at_x = pl.ds(pl.multiple_of(step * flip_rows + SHIFTS * LINES, flip_rows), flip_rows)
        xjf[at, :] = jnp.dot(xf[at_x, :].astype(BF), turn, preferred_element_type=F32)
        return carry

    lax.fori_loop(0, blocks // 4, flip, 0)
    last = slice(blocks * LINES, (blocks + SHIFTS) * LINES)
    cjf[last, :] = jnp.dot(cf[last, :].astype(BF), turn, preferred_element_type=F32)

    ins[2].wait()
    arrived(rq_in, rq_sem)
    asked = rq_in[...].reshape(chips, BANK_ROWS)
    first = one_hot((asked == 1.0) | (asked == 3.0))
    second = one_hot(asked >= 2.0)
    owned[...] = jnp.concatenate([first, second], axis=0).astype(BF)

    def pack_slots(values, out_ref):
        for slot in range(SLOTS):
            for s in range(SHIFTS):
                stage[pl.ds(slot * SHIFTS + s, chips, stride=SLOTS * SHIFTS), :] = values[
                    slot * chips : (slot + 1) * chips, s * LANES : (s + 1) * LANES
                ]
        out_ref[...] = stage[...].reshape(chips, SLOTS * SHIFTS, LANES).astype(BF)

    def unpack_slots(in_ref):
        stage[...] = in_ref[...].astype(F32).reshape(chips * SLOTS * SHIFTS, LANES)
        return jnp.concatenate(
            [
                jnp.concatenate(
                    [
                        stage[pl.ds(slot * SHIFTS + s, chips, stride=SLOTS * SHIFTS), :]
                        for s in range(SHIFTS)
                    ],
                    axis=1,
                )
                for slot in range(SLOTS)
            ],
            axis=0,
        ).astype(BF)

    pack_slots(jnp.dot(owned[...], bank[...], preferred_element_type=F32), fe_out)
    scatter(fe_out, fe_in, fe_sem)

    across = iota((LANES, LANES), 0) + iota((LANES, LANES), 1) >= LANES - 1

    def lag_line(line):
        here = xjf[pl.ds(line, blocks, stride=LINES), :].astype(BF)
        later = jnp.concatenate(
            [
                cf[pl.ds(s * LINES + line, blocks, stride=LINES), :].astype(BF)
                for s in range(SHIFTS + 1)
            ],
            axis=1,
        )
        prod = lax.dot_general(
            here, later, (((0,), (0,)), ((), ())), preferred_element_type=F32
        )
        for s in range(SHIFTS):
            part = jnp.where(
                across,
                prod[:, s * LANES : (s + 1) * LANES],
                prod[:, (s + 1) * LANES : (s + 2) * LANES],
            )
            part = pltpu.roll(part, 1, 1, stride=1, stride_axis=0)
            part = jnp.sum(part.reshape(LANES // 8, 8, LANES), axis=0)
            acc[s, pl.ds(pl.multiple_of(line * 8, 8), 8), :] = part

    def windows(line):
        for s in range(SHIFTS + 1):
            span = slice(s * LANES, (s + 1) * LANES)
            lhs[line, 0:blocks, span] = xf[
                pl.ds((SHIFTS - s) * LINES + line, blocks, stride=LINES), :
            ].astype(BF)
            lhs[line, blocks : 2 * blocks, span] = cjf[
                pl.ds(s * LINES + line, blocks, stride=LINES), :
            ].astype(BF)

    def before(step, carry):
        for u in range(2):
            lag_line(step * 2 + u)
            windows(step * 2 + u)
        return carry

    lax.fori_loop(0, LINES // 2, before, 0)
    scale = 1.0 / math.sqrt(2 * blocks * LANES)
    lag = jnp.concatenate(
        [
            sum(acc[s, pl.ds(r, LINES, stride=8), :] for r in range(8))
            for s in range(SHIFTS)
        ],
        axis=1,
    )
    lx_out[...] = jnp.where(tap_mask, lag, 0.0) * scale
    lag_swap = swap(lx_out, lx_in, lx_sem)
    lag_swap.start()
    lag_swap.wait_recv()
    lag = (lx_out[...] + lx_in[...]).astype(BF)
    pack_slots(jnp.dot(pick_t, lag, preferred_element_type=F32), re_out)
    scatter(re_out, re_in, re_sem)

    arrived(fe_in, fe_sem)
    mine = jnp.dot(pick, unpack_slots(fe_in), preferred_element_type=F32)
    kx_out[...] = jnp.where(tap_mask, mine, 0.0).astype(BF)
    tap_swap = swap(kx_out, kx_in, kx_sem)
    tap_swap.start()
    tap_swap.wait_recv()
    taps = kx_out[...].astype(F32) + kx_in[...].astype(F32)
    for s in range(SHIFTS):
        kf[s * LINES : (s + 1) * LINES, :] = taps[:, s * LANES : (s + 1) * LANES]

    upper = iota((LANES, LANES), 1) >= iota((LANES, LANES), 0)

    def filter_line(line):
        bands = []
        before_it = jnp.zeros((LANES, LANES), F32)
        for s in range(SHIFTS):
            row = kf[pl.ds(s * LINES + line, 1), :]
            rolled = pltpu.roll(
                jnp.broadcast_to(row, (LANES, LANES)), 0, 1, stride=1, stride_axis=0
            )
            bands.append(jnp.where(upper, rolled, before_it).astype(BF))
            before_it = rolled
        bands.append(jnp.where(upper, 0.0, before_it).astype(BF))
        both = jnp.dot(
            lhs[line], jnp.concatenate(bands, axis=0), preferred_element_type=F32
        )
        of[pl.ds(line, blocks, stride=LINES), :] = both[:blocks]
        gf[pl.ds(line, blocks, stride=LINES), :] = both[blocks:]

    def filters(half):
        def step_of(step, carry):
            for u in range(2):
                filter_line(half * 16 + step * 2 + u)
            return carry

        lax.fori_loop(0, 8, step_of, 0)
        copies = []
        at = slice(half * 16, half * 16 + 16)
        for q in range(blocks):
            span = slice(q * LANES, (q + 1) * LANES)
            from_ = slice(q * LINES + half * 16, q * LINES + half * 16 + 16)
            fil[at, span] = of[from_, :].astype(BF)
            grad[at, span] = jnp.dot(
                gf[from_, :].astype(BF), turn, preferred_element_type=F32
            ).astype(BF)
        copies = [
            pltpu.make_async_copy(fil.at[at], fil_hbm.at[at], out_sem.at[2 * half]),
            pltpu.make_async_copy(grad.at[at], grad_hbm.at[at], out_sem.at[2 * half + 1]),
        ]
        for copy in copies:
            copy.start()
        return copies

    outs = filters(0)

    arrived(re_in, re_sem)
    total = lax.dot_general(
        owned[...], unpack_slots(re_in), (((0,), (0,)), ((), ())), preferred_element_type=F32
    )
    half_taps = TAPS // 2
    gx_out[...] = jnp.where(core == 0, total[:, half_taps:], total[:, :half_taps])
    bgrad[...] = jnp.where(core == 0, total[:, :half_taps], total[:, half_taps:])
    sum_swap = swap(gx_out, gx_in, gx_sem)
    sum_swap.start()

    outs = outs + filters(1)
    sum_swap.wait_recv()
    bgrad[...] = bgrad[...] + gx_in[...]
    outs.append(pltpu.make_async_copy(bgrad, bgrad_hbm, out_sem.at[4]))
    outs[-1].start()

    pltpu.make_async_copy(halo, halo, halo_sem.at[0]).wait()
    departed(rq_out, rq_sem)
    departed(fe_out, fe_sem)
    departed(re_out, re_sem)
    lag_swap.wait_send()
    tap_swap.wait_send()
    sum_swap.wait_send()
    for copy in outs:
        copy.wait()


def body(signal, cotangent, bank, lengths, kernel_ids):
    line_count, samples = signal.shape
    blocks = samples // LANES
    chips = lax.axis_size("line") // 2
    any_ = pl.BlockSpec(memory_space=pl.ANY)
    vmem = pl.BlockSpec(memory_space=pltpu.VMEM)
    message = (chips, SLOTS * SHIFTS, LANES)
    pair = pltpu.SemaphoreType.DMA((2,))
    return pl.pallas_call(
        kernel,
        out_shape=(
            jax.ShapeDtypeStruct((line_count, samples), BF),
            jax.ShapeDtypeStruct((line_count, samples), BF),
            jax.ShapeDtypeStruct((BANK_ROWS, TAPS // 2), F32),
        ),
        in_specs=[any_, any_, any_, vmem, vmem],
        out_specs=(any_, any_, any_),
        scratch_shapes=[
            pltpu.VMEM((line_count, samples), BF),
            pltpu.VMEM((line_count, samples), BF),
            pltpu.VMEM((BANK_ROWS, TAPS), BF),
            pltpu.VMEM((line_count, samples), BF),
            pltpu.VMEM((line_count, samples), BF),
            pltpu.VMEM((BANK_ROWS, TAPS // 2), F32),
            pltpu.VMEM((line_count, TAPS), BF),
            pltpu.VMEM((chips, 1, LANES), F32),
            pltpu.VMEM((chips, 1, LANES), F32),
            pltpu.VMEM(message, BF),
            pltpu.VMEM(message, BF),
            pltpu.VMEM(message, BF),
            pltpu.VMEM(message, BF),
            pltpu.VMEM((line_count, TAPS), BF),
            pltpu.VMEM((line_count, TAPS), BF),
            pltpu.VMEM((line_count, TAPS), F32),
            pltpu.VMEM((line_count, TAPS), F32),
            pltpu.VMEM((BANK_ROWS, TAPS // 2), F32),
            pltpu.VMEM((BANK_ROWS, TAPS // 2), F32),
            pltpu.VMEM(((blocks + SHIFTS) * line_count, LANES), F32),
            pltpu.VMEM(((blocks + SHIFTS) * line_count, LANES), F32),
            pltpu.VMEM(((blocks + SHIFTS) * line_count, LANES), F32),
            pltpu.VMEM((blocks * line_count, LANES), F32),
            pltpu.VMEM((line_count, 2 * blocks, TAPS + LANES), BF),
            pltpu.VMEM((SHIFTS, 8 * line_count, LANES), F32),
            pltpu.VMEM((SHIFTS * line_count, LANES), F32),
            pltpu.VMEM((chips * SLOTS * SHIFTS, LANES), F32),
            pltpu.VMEM((SLOTS * chips, BANK_ROWS), BF),
            pltpu.VMEM((blocks * line_count, LANES), F32),
            pltpu.VMEM((blocks * line_count, LANES), F32),
            pltpu.SemaphoreType.DMA((3,)),
            pltpu.SemaphoreType.DMA((5,)),
            pair, pair, pair, pair, pair, pair, pair,
        ],
        compiler_params=pltpu.CompilerParams(
            collective_id=0, has_side_effects=True, vmem_limit_bytes=48 * 1024 * 1024
        ),
        cost_estimate=pl.CostEstimate(
            flops=6 * line_count * samples * TAPS, bytes_accessed=1 << 21, transcendentals=0
        ),
    )(signal, cotangent, bank, lengths, kernel_ids)


def solution(mesh):
    return jax.shard_map(
        body,
        mesh=mesh,
        in_specs=(P("line", "tm"), P("line", "tm"), P("line", None), P("line"), P("line")),
        out_specs=(P("line", "tm"), P("line", "tm"), P("line", "tm")),
        check_vma=False,
    )
```

```python
import math

import jax
import jax.numpy as jnp
from jax import lax
from jax.experimental import pallas as pl
from jax.experimental.pallas import tpu as pltpu
from jax.sharding import PartitionSpec as P

MESH = pl.DeviceIdType.MESH
BF = jnp.bfloat16
F32 = jnp.float32
LINES = 32
TAPS = 512
LANES = 128
SHIFTS = TAPS // LANES
SLOTS = 2
BANK_ROWS = 128
PITCH = LINES + 1


def iota(shape, dim):
    return lax.broadcasted_iota(jnp.int32, shape, dim)


def column(row):
    size = row.shape[1]
    mask = iota((size, size), 0) == iota((size, size), 1)
    return jnp.sum(jnp.where(mask, jnp.broadcast_to(row, (size, size)), 0.0), axis=1, keepdims=True)


def one_hot(hit):
    return jnp.where(hit, 1.0, 0.0)


def kernel(
    sig_hbm, cot_hbm, bank_hbm, len_hbm, ids_hbm,
    fil, grad, bgrad,
    sig, cot, bank, len_ref, ids_ref,
    halo, rq_out, rq_in, fe_out, fe_in, re_out, re_in,
    kx_out, kx_in, lx_out, lx_in, gx_out, gx_in,
    xf, cf, cjf, xjf, lhs, acc, kf, stage, owned, of, gf,
    in_sem, halo_sem, rq_sem, fe_sem, re_sem, kx_sem, lx_sem, gx_sem,
):
    me = lax.axis_index("line")
    core = lax.axis_index("tm")
    other = (me, 1 - core)
    blocks = sig.shape[1] // LANES
    chips = rq_out.shape[0]
    par = lax.rem(me + core, 2)
    place = lax.div(me, 2)
    here_z = lax.rem(place, 4)
    here_y = lax.rem(lax.div(place, 4), 4)
    here_x = lax.div(place, 16)

    ins = [
        pltpu.make_async_copy(ids_hbm, ids_ref, in_sem.at[0]),
        pltpu.make_async_copy(len_hbm, len_ref, in_sem.at[1]),
        pltpu.make_async_copy(sig_hbm, sig, in_sem.at[2]),
        pltpu.make_async_copy(cot_hbm, cot, in_sem.at[3]),
        pltpu.make_async_copy(bank_hbm, bank, in_sem.at[4]),
    ]
    for copy in ins:
        copy.start()

    def peer(step):
        a = step // 16
        b = (step // 4) % 4
        c = step % 4
        z = lax.rem(here_z + 2 + (a * (a + 1)) // 2, 4)
        x = lax.rem(here_x + 2 + (b * (b + 1)) // 2, 4)
        y = lax.rem(here_y + 2 + (c * (c + 1)) // 2, 4)
        return x * 16 + y * 4 + z

    barrier = pltpu.get_barrier_semaphore()

    def greet(step, carry):
        pl.semaphore_signal(
            barrier, inc=1, device_id=(2 * peer(step) + par, core), device_id_type=MESH
        )
        return carry

    lax.fori_loop(0, chips - 1, greet, 0, unroll=9)

    @pl.when(core == 1)
    def _():
        pl.semaphore_signal(barrier, inc=1, device_id=(2 * place + par, core), device_id_type=MESH)

    pl.semaphore_signal(barrier, inc=1, device_id=other, device_id_type=MESH)

    def scatter(out_ref, in_ref, sems):
        def send(step, carry):
            i = peer(step)
            pltpu.make_async_remote_copy(
                src_ref=out_ref.at[i],
                dst_ref=in_ref.at[place],
                send_sem=sems.at[0],
                recv_sem=sems.at[1],
                device_id=(2 * i + par, core),
                device_id_type=MESH,
            ).start()
            return carry

        lax.fori_loop(0, chips - 1, send, 0, unroll=9)

        @pl.when(core == 1)
        def _():
            pltpu.make_async_remote_copy(
                src_ref=out_ref.at[place],
                dst_ref=in_ref.at[place],
                send_sem=sems.at[0],
                recv_sem=sems.at[1],
                device_id=(2 * place + par, core),
                device_id_type=MESH,
            ).start()

        @pl.when(core == 0)
        def _():
            pltpu.make_async_copy(out_ref.at[place], in_ref.at[place], sems.at[1]).start()

    def arrived(in_ref, sems):
        pltpu.make_async_copy(in_ref, in_ref, sems.at[1]).wait()

    def departed(out_ref, sems):
        part = out_ref.at[pl.ds(0, chips - 1)]
        pltpu.make_async_copy(part, part, sems.at[0]).wait()

        @pl.when(core == 1)
        def _():
            pltpu.make_async_copy(out_ref.at[0], out_ref.at[0], sems.at[0]).wait()

    def swap(out_ref, in_ref, sems):
        return pltpu.make_async_remote_copy(
            src_ref=out_ref,
            dst_ref=in_ref,
            send_sem=sems.at[0],
            recv_sem=sems.at[1],
            device_id=other,
            device_id_type=MESH,
        )

    for copy in ins[:2]:
        copy.wait()
    ids_row = ids_ref[...].reshape(1, LINES)
    holder_row = ids_row // BANK_ROWS
    inside_row = ids_row % BANK_ROWS
    holder_col = column(holder_row.astype(F32)).astype(jnp.int32)
    inside_col = column(inside_row.astype(F32)).astype(jnp.int32)
    len_col = column(len_ref[...].reshape(1, LINES).astype(F32)).astype(jnp.int32)
    same = jnp.broadcast_to(holder_col, (LINES, LINES)) == jnp.broadcast_to(holder_row, (LINES, LINES))
    subs = iota((LINES, LINES), 0)
    lanes = iota((LINES, LINES), 1)
    rank_col = jnp.sum(one_hot(same & (lanes < subs)), axis=1, keepdims=True).astype(jnp.int32)
    rank_row = jnp.sum(one_hot(same & (subs < lanes)), axis=0, keepdims=True).astype(jnp.int32)
    spot_col = jnp.where(holder_col % 2 == par, holder_col // 2, -chips * SLOTS)
    spot_row = jnp.where(holder_row % 2 == par, holder_row // 2, -chips * SLOTS)
    picks = SLOTS * chips
    pick = one_hot(iota((LINES, picks), 1) == spot_col + rank_col * chips).astype(BF)
    pick_t = one_hot(iota((picks, LINES), 0) == spot_row + rank_row * chips).astype(BF)
    wanted = jnp.where(
        iota((chips, LINES), 0) == spot_row, (rank_row + 1).astype(F32), 0.0
    ).astype(BF)
    rows = one_hot(iota((LINES, BANK_ROWS), 1) == inside_col).astype(BF)
    asks = jnp.dot(wanted, rows, preferred_element_type=F32)
    rq_out[...] = asks.reshape(chips, 1, BANK_ROWS)
    tap_mask = iota((LINES, TAPS), 1) < len_col

    for copy in ins[2:4]:
        copy.wait()
    turn = one_hot(iota((LANES, LANES), 0) + iota((LANES, LANES), 1) == LANES - 1).astype(BF)
    for q in range(blocks):
        span = slice(q * LANES, (q + 1) * LANES)
        at = slice(q * PITCH, q * PITCH + LINES)
        xf[(SHIFTS + q) * PITCH : (SHIFTS + q) * PITCH + LINES, :] = sig[:, span].astype(F32)
        cf[at, :] = cot[:, span].astype(F32)
        xjf[at, :] = jnp.dot(sig[:, span], turn, preferred_element_type=F32)
        cjf[at, :] = jnp.dot(cot[:, span], turn, preferred_element_type=F32)
    pl.semaphore_wait(barrier, chips + core)

    scatter(rq_out, rq_in, rq_sem)

    @pl.when(core == 0)
    def _():
        swap(sig.at[:, pl.ds(blocks * LANES - TAPS, TAPS)], halo, halo_sem).start()

    @pl.when(core == 1)
    def _():
        swap(cot.at[:, pl.ds(0, TAPS)], halo, halo_sem).start()

    pltpu.make_async_copy(halo, halo, halo_sem.at[1]).wait()
    for s in range(SHIFTS):
        edge = halo[:, s * LANES : (s + 1) * LANES]
        before_it = jnp.where(core == 1, edge.astype(F32), 0.0)
        after_it = jnp.where(core == 0, edge.astype(F32), 0.0)
        at = slice((blocks + s) * PITCH, (blocks + s) * PITCH + LINES)
        xf[s * PITCH : s * PITCH + LINES, :] = before_it
        cf[at, :] = after_it
        cjf[at, :] = jnp.dot(after_it.astype(BF), turn, preferred_element_type=F32)

    across = iota((LANES, LANES), 0) + iota((LANES, LANES), 1) >= LANES - 1

    def lag_line(line):
        here = xjf[pl.ds(line, blocks, stride=PITCH), :].astype(BF)
        later = jnp.concatenate(
            [
                cf[pl.ds(s * PITCH + line, blocks, stride=PITCH), :].astype(BF)
                for s in range(SHIFTS + 1)
            ],
            axis=1,
        )
        prod = lax.dot_general(
            here, later, (((0,), (0,)), ((), ())), preferred_element_type=F32
        )
        for s in range(SHIFTS):
            part = jnp.where(
                across,
                prod[:, s * LANES : (s + 1) * LANES],
                prod[:, (s + 1) * LANES : (s + 2) * LANES],
            )
            part = pltpu.roll(part, 1, 1, stride=1, stride_axis=0)
            part = jnp.sum(part.reshape(LANES // 8, 8, LANES), axis=0)
            acc[s, pl.ds(pl.multiple_of(line * 8, 8), 8), :] = part

    def windows(line):
        for s in range(SHIFTS + 1):
            span = slice(s * LANES, (s + 1) * LANES)
            lhs[line, 0:blocks, span] = xf[
                pl.ds((SHIFTS - s) * PITCH + line, blocks, stride=PITCH), :
            ].astype(BF)
            lhs[line, blocks : 2 * blocks, span] = cjf[
                pl.ds(s * PITCH + line, blocks, stride=PITCH), :
            ].astype(BF)

    def before(step, carry):
        for u in range(8):
            lag_line(step * 8 + u)
        return carry

    lax.fori_loop(0, LINES // 8, before, 0)
    scale = 1.0 / math.sqrt(2 * blocks * LANES)
    lag = jnp.concatenate(
        [
            sum(acc[s, pl.ds(r, LINES, stride=8), :] for r in range(8))
            for s in range(SHIFTS)
        ],
        axis=1,
    )
    lx_out[...] = jnp.where(tap_mask, lag, 0.0) * scale
    lag_swap = swap(lx_out, lx_in, lx_sem)
    lag_swap.start()
    ins[4].wait()
    arrived(rq_in, rq_sem)
    asked = rq_in[...].reshape(chips, BANK_ROWS)
    first = one_hot((asked == 1.0) | (asked == 3.0))
    second = one_hot(asked >= 2.0)
    owned[...] = jnp.concatenate([first, second], axis=0).astype(BF)

    def pack_slots(values, out_ref):
        for slot in range(SLOTS):
            for s in range(SHIFTS):
                stage[pl.ds(slot * SHIFTS + s, chips, stride=SLOTS * SHIFTS), :] = values[
                    slot * chips : (slot + 1) * chips, s * LANES : (s + 1) * LANES
                ]
        out_ref[...] = stage[...].reshape(chips, SLOTS * SHIFTS, LANES).astype(BF)

    def unpack_slots(in_ref):
        stage[...] = in_ref[...].astype(F32).reshape(chips * SLOTS * SHIFTS, LANES)
        return jnp.concatenate(
            [
                jnp.concatenate(
                    [
                        stage[pl.ds(slot * SHIFTS + s, chips, stride=SLOTS * SHIFTS), :]
                        for s in range(SHIFTS)
                    ],
                    axis=1,
                )
                for slot in range(SLOTS)
            ],
            axis=0,
        ).astype(BF)

    pack_slots(jnp.dot(owned[...], bank[...], preferred_element_type=F32), fe_out)
    scatter(fe_out, fe_in, fe_sem)

    def prepare(step, carry):
        for u in range(2):
            windows(step * 2 + u)
        return carry

    lag_swap.wait_recv()
    lag = (lx_out[...] + lx_in[...]).astype(BF)
    pack_slots(jnp.dot(pick_t, lag, preferred_element_type=F32), re_out)
    scatter(re_out, re_in, re_sem)
    lax.fori_loop(0, LINES // 2, prepare, 0)


    arrived(fe_in, fe_sem)
    mine = jnp.dot(pick, unpack_slots(fe_in), preferred_element_type=F32)
    kx_out[...] = jnp.where(tap_mask, mine, 0.0).astype(BF)
    tap_swap = swap(kx_out, kx_in, kx_sem)
    tap_swap.start()
    tap_swap.wait_recv()
    taps = kx_out[...].astype(F32) + kx_in[...].astype(F32)
    for s in range(SHIFTS):
        kf[s * LINES : (s + 1) * LINES, :] = taps[:, s * LANES : (s + 1) * LANES]

    upper = iota((LANES, LANES), 1) >= iota((LANES, LANES), 0)

    def filter_line(line):
        bands = []
        before_it = jnp.zeros((LANES, LANES), F32)
        for s in range(SHIFTS):
            row = kf[pl.ds(s * LINES + line, 1), :]
            rolled = pltpu.roll(
                jnp.broadcast_to(row, (LANES, LANES)), 0, 1, stride=1, stride_axis=0
            )
            bands.append(jnp.where(upper, rolled, before_it).astype(BF))
            before_it = rolled
        bands.append(jnp.where(upper, 0.0, before_it).astype(BF))
        both = jnp.dot(
            lhs[line], jnp.concatenate(bands, axis=0), preferred_element_type=F32
        )
        of[pl.ds(line, blocks, stride=PITCH), :] = both[:blocks]
        gf[pl.ds(line, blocks, stride=PITCH), :] = both[blocks:]

    def filters(half):
        def step_of(step, carry):
            for u in range(16):
                filter_line(half * 16 + step * 16 + u)
            return carry

        lax.fori_loop(0, 1, step_of, 0)
        at = slice(half * 16, half * 16 + 16)
        for q in range(blocks):
            span = slice(q * LANES, (q + 1) * LANES)
            from_ = slice(q * PITCH + half * 16, q * PITCH + half * 16 + 16)
            fil[at, span] = of[from_, :].astype(BF)
            grad[at, span] = jnp.dot(
                gf[from_, :].astype(BF), turn, preferred_element_type=F32
            ).astype(BF)

    filters(0)

    arrived(re_in, re_sem)
    total = lax.dot_general(
        owned[...], unpack_slots(re_in), (((0,), (0,)), ((), ())), preferred_element_type=F32
    )
    half_taps = TAPS // 2
    gx_out[...] = jnp.where(core == 0, total[:, half_taps:], total[:, :half_taps])
    bgrad[...] = jnp.where(core == 0, total[:, :half_taps], total[:, half_taps:])
    sum_swap = swap(gx_out, gx_in, gx_sem)
    sum_swap.start()

    filters(1)
    sum_swap.wait_recv()
    bgrad[...] = bgrad[...] + gx_in[...]

    pltpu.make_async_copy(halo, halo, halo_sem.at[0]).wait()
    departed(rq_out, rq_sem)
    departed(fe_out, fe_sem)
    departed(re_out, re_sem)
    lag_swap.wait_send()
    tap_swap.wait_send()
    sum_swap.wait_send()


def finish(fil, grad, bgrad, fil_hbm, grad_hbm, bgrad_hbm, sem):
    outs = [
        pltpu.make_async_copy(fil, fil_hbm, sem.at[0]),
        pltpu.make_async_copy(grad, grad_hbm, sem.at[1]),
        pltpu.make_async_copy(bgrad, bgrad_hbm, sem.at[2]),
    ]
    for copy in outs:
        copy.start()
    for copy in outs:
        copy.wait()


def body(signal, cotangent, bank, lengths, kernel_ids):
    line_count, samples = signal.shape
    blocks = samples // LANES
    chips = lax.axis_size("line") // 2
    any_ = pl.BlockSpec(memory_space=pl.ANY)
    vmem = pl.BlockSpec(memory_space=pltpu.VMEM)
    message = (chips, SLOTS * SHIFTS, LANES)
    pair = pltpu.SemaphoreType.DMA((2,))
    shapes = (
        ((line_count, samples), BF),
        ((line_count, samples), BF),
        ((BANK_ROWS, TAPS // 2), F32),
    )
    results = pl.pallas_call(
        kernel,
        out_shape=tuple(pltpu.VMEM(*shape) for shape in shapes),
        in_specs=[any_] * 5,
        out_specs=(vmem,) * 3,
        scratch_shapes=[
            pltpu.VMEM((line_count, samples), BF),
            pltpu.VMEM((line_count, samples), BF),
            pltpu.VMEM((BANK_ROWS, TAPS), BF),
            pltpu.VMEM((line_count,), jnp.int32),
            pltpu.VMEM((line_count,), jnp.int32),
            pltpu.VMEM((line_count, TAPS), BF),
            pltpu.VMEM((chips, 1, LANES), F32),
            pltpu.VMEM((chips, 1, LANES), F32),
            pltpu.VMEM(message, BF),
            pltpu.VMEM(message, BF),
            pltpu.VMEM(message, BF),
            pltpu.VMEM(message, BF),
            pltpu.VMEM((line_count, TAPS), BF),
            pltpu.VMEM((line_count, TAPS), BF),
            pltpu.VMEM((line_count, TAPS), F32),
            pltpu.VMEM((line_count, TAPS), F32),
            pltpu.VMEM((BANK_ROWS, TAPS // 2), F32),
            pltpu.VMEM((BANK_ROWS, TAPS // 2), F32),
            pltpu.VMEM(((blocks + SHIFTS) * PITCH, LANES), F32),
            pltpu.VMEM(((blocks + SHIFTS) * PITCH, LANES), F32),
            pltpu.VMEM(((blocks + SHIFTS) * PITCH, LANES), F32),
            pltpu.VMEM((blocks * PITCH, LANES), F32),
            pltpu.VMEM((line_count, 2 * blocks, TAPS + LANES), BF),
            pltpu.VMEM((SHIFTS, 8 * line_count, LANES), F32),
            pltpu.VMEM((SHIFTS * line_count, LANES), F32),
            pltpu.VMEM((chips * SLOTS * SHIFTS, LANES), F32),
            pltpu.VMEM((SLOTS * chips, BANK_ROWS), BF),
            pltpu.VMEM((blocks * PITCH, LANES), F32),
            pltpu.VMEM((blocks * PITCH, LANES), F32),
            pltpu.SemaphoreType.DMA((5,)),
            pair, pair, pair, pair, pair, pair, pair,
        ],
        compiler_params=pltpu.CompilerParams(
            collective_id=0, has_side_effects=True, vmem_limit_bytes=60 * 1024 * 1024
        ),
        cost_estimate=pl.CostEstimate(
            flops=6 * line_count * samples * TAPS, bytes_accessed=1 << 21, transcendentals=0
        ),
    )(signal, cotangent, bank, lengths, kernel_ids)
    return pl.pallas_call(
        finish,
        out_shape=tuple(jax.ShapeDtypeStruct(*shape) for shape in shapes),
        in_specs=[vmem] * 3,
        out_specs=(any_,) * 3,
        scratch_shapes=[pltpu.SemaphoreType.DMA((3,))],
    )(*[pltpu.with_memory_space_constraint(r, pltpu.VMEM) for r in results])


def solution(mesh):
    return jax.shard_map(
        body,
        mesh=mesh,
        in_specs=(P("line", "tm"), P("line", "tm"), P("line", None), P("line"), P("line")),
        out_specs=(P("line", "tm"), P("line", "tm"), P("line", "tm")),
        check_vma=False,
    )
```

```python
import math

import jax
import jax.numpy as jnp
from jax import lax
from jax.experimental import pallas as pl
from jax.experimental.pallas import tpu as pltpu
from jax.sharding import PartitionSpec as P

MESH = pl.DeviceIdType.MESH
BF = jnp.bfloat16
F32 = jnp.float32
LINES = 32
TAPS = 512
LANES = 128
SHIFTS = TAPS // LANES
SLOTS = 2
ROWS = SLOTS * SHIFTS
BANK_ROWS = 128
PITCH = LINES + 1
STEP = ROWS + 1


def iota(shape, dim):
    return lax.broadcasted_iota(jnp.int32, shape, dim)


def column(row):
    size = row.shape[1]
    mask = iota((size, size), 0) == iota((size, size), 1)
    return jnp.sum(jnp.where(mask, jnp.broadcast_to(row, (size, size)), 0.0), axis=1, keepdims=True)


def one_hot(hit):
    return jnp.where(hit, 1.0, 0.0)


def kernel(
    sig_hbm, cot_hbm, bank_hbm, len_hbm, ids_hbm,
    fil, grad, bgrad,
    sig, cot, bank, len_ref, ids_ref,
    halo, rq_out, rq_in, fe_out, fe_in, re_out, re_in,
    kx_out, kx_in, lx_out, lx_in, gx_out, gx_in,
    xf, cf, cjf, xjf, lhs, acc, kf, stage, owned, of, gf,
    in_sem, halo_sem, rq_sem, fe_sem, re_sem, kx_sem, lx_sem, gx_sem,
):
    me = lax.axis_index("line")
    core = lax.axis_index("tm")
    other = (me, 1 - core)
    blocks = sig.shape[1] // LANES
    chips = rq_out.shape[0]
    par = lax.rem(me + core, 2)
    place = lax.div(me, 2)
    here_z = lax.rem(place, 4)
    here_y = lax.rem(lax.div(place, 4), 4)
    here_x = lax.div(place, 16)

    ins = [
        pltpu.make_async_copy(ids_hbm, ids_ref, in_sem.at[0]),
        pltpu.make_async_copy(len_hbm, len_ref, in_sem.at[1]),
        pltpu.make_async_copy(sig_hbm, sig, in_sem.at[2]),
        pltpu.make_async_copy(cot_hbm, cot, in_sem.at[3]),
        pltpu.make_async_copy(bank_hbm, bank, in_sem.at[4]),
    ]
    for copy in ins:
        copy.start()

    def peer(step):
        a = step // 16
        b = (step // 4) % 4
        c = step % 4
        z = lax.rem(here_z + 2 + (a * (a + 1)) // 2, 4)
        x = lax.rem(here_x + 2 + (b * (b + 1)) // 2, 4)
        y = lax.rem(here_y + 2 + (c * (c + 1)) // 2, 4)
        return x * 16 + y * 4 + z

    barrier = pltpu.get_barrier_semaphore()

    def greet(step, carry):
        pl.semaphore_signal(
            barrier, inc=1, device_id=(2 * peer(step) + par, core), device_id_type=MESH
        )
        return carry

    lax.fori_loop(0, chips - 1, greet, 0, unroll=9)

    @pl.when(core == 1)
    def _():
        pl.semaphore_signal(barrier, inc=1, device_id=(2 * place + par, core), device_id_type=MESH)

    pl.semaphore_signal(barrier, inc=1, device_id=other, device_id_type=MESH)

    def scatter(out_ref, in_ref, sems):
        def send(step, carry):
            i = peer(step)
            pltpu.make_async_remote_copy(
                src_ref=out_ref.at[i],
                dst_ref=in_ref.at[place],
                send_sem=sems.at[0],
                recv_sem=sems.at[1],
                device_id=(2 * i + par, core),
                device_id_type=MESH,
            ).start()
            return carry

        lax.fori_loop(0, chips - 1, send, 0, unroll=9)

        @pl.when(core == 1)
        def _():
            pltpu.make_async_remote_copy(
                src_ref=out_ref.at[place],
                dst_ref=in_ref.at[place],
                send_sem=sems.at[0],
                recv_sem=sems.at[1],
                device_id=(2 * place + par, core),
                device_id_type=MESH,
            ).start()

        @pl.when(core == 0)
        def _():
            pltpu.make_async_copy(out_ref.at[place], in_ref.at[place], sems.at[1]).start()

    def arrived(in_ref, sems):
        pltpu.make_async_copy(in_ref, in_ref, sems.at[1]).wait()

    def departed(out_ref, sems):
        part = out_ref.at[pl.ds(0, chips - 1)]
        pltpu.make_async_copy(part, part, sems.at[0]).wait()

        @pl.when(core == 1)
        def _():
            pltpu.make_async_copy(out_ref.at[0], out_ref.at[0], sems.at[0]).wait()

    def swap(out_ref, in_ref, sems):
        return pltpu.make_async_remote_copy(
            src_ref=out_ref,
            dst_ref=in_ref,
            send_sem=sems.at[0],
            recv_sem=sems.at[1],
            device_id=other,
            device_id_type=MESH,
        )

    for copy in ins[:2]:
        copy.wait()
    ids_row = ids_ref[...].reshape(1, LINES)
    holder_row = ids_row // BANK_ROWS
    inside_row = ids_row % BANK_ROWS
    holder_col = column(holder_row.astype(F32)).astype(jnp.int32)
    inside_col = column(inside_row.astype(F32)).astype(jnp.int32)
    len_col = column(len_ref[...].reshape(1, LINES).astype(F32)).astype(jnp.int32)
    same = jnp.broadcast_to(holder_col, (LINES, LINES)) == jnp.broadcast_to(holder_row, (LINES, LINES))
    subs = iota((LINES, LINES), 0)
    lanes = iota((LINES, LINES), 1)
    rank_col = jnp.sum(one_hot(same & (lanes < subs)), axis=1, keepdims=True).astype(jnp.int32)
    rank_row = jnp.sum(one_hot(same & (subs < lanes)), axis=0, keepdims=True).astype(jnp.int32)
    spot_col = jnp.where(holder_col % 2 == par, holder_col // 2, -chips * SLOTS)
    spot_row = jnp.where(holder_row % 2 == par, holder_row // 2, -chips * SLOTS)
    picks = SLOTS * chips
    pick = one_hot(iota((LINES, picks), 1) == spot_col + rank_col * chips).astype(BF)
    pick_t = one_hot(iota((picks, LINES), 0) == spot_row + rank_row * chips).astype(BF)
    wanted = jnp.where(
        iota((chips, LINES), 0) == spot_row, (rank_row + 1).astype(F32), 0.0
    ).astype(BF)
    rows = one_hot(iota((LINES, BANK_ROWS), 1) == inside_col).astype(BF)
    asks = jnp.dot(wanted, rows, preferred_element_type=F32)
    rq_out[...] = asks.reshape(chips, 1, BANK_ROWS)
    tap_mask = iota((LINES, TAPS), 1) < len_col

    for copy in ins[2:4]:
        copy.wait()
    turn = one_hot(iota((LANES, LANES), 0) + iota((LANES, LANES), 1) == LANES - 1).astype(BF)
    for q in range(blocks):
        span = slice(q * LANES, (q + 1) * LANES)
        at = slice(q * PITCH, q * PITCH + LINES)
        xf[(SHIFTS + q) * PITCH : (SHIFTS + q) * PITCH + LINES, :] = sig[:, span].astype(F32)
        cf[at, :] = cot[:, span].astype(F32)
        xjf[at, :] = jnp.dot(sig[:, span], turn, preferred_element_type=F32)
        cjf[at, :] = jnp.dot(cot[:, span], turn, preferred_element_type=F32)
    pl.semaphore_wait(barrier, chips + core)

    scatter(rq_out, rq_in, rq_sem)

    @pl.when(core == 0)
    def _():
        swap(sig.at[:, pl.ds(blocks * LANES - TAPS, TAPS)], halo, halo_sem).start()

    @pl.when(core == 1)
    def _():
        swap(cot.at[:, pl.ds(0, TAPS)], halo, halo_sem).start()

    pltpu.make_async_copy(halo, halo, halo_sem.at[1]).wait()
    for s in range(SHIFTS):
        edge = halo[:, s * LANES : (s + 1) * LANES]
        before_it = jnp.where(core == 1, edge.astype(F32), 0.0)
        after_it = jnp.where(core == 0, edge.astype(F32), 0.0)
        at = slice((blocks + s) * PITCH, (blocks + s) * PITCH + LINES)
        xf[s * PITCH : s * PITCH + LINES, :] = before_it
        cf[at, :] = after_it
        cjf[at, :] = jnp.dot(after_it.astype(BF), turn, preferred_element_type=F32)

    across = iota((LANES, LANES), 0) + iota((LANES, LANES), 1) >= LANES - 1

    def lag_line(line):
        here = xjf[pl.ds(line, blocks, stride=PITCH), :].astype(BF)
        later = jnp.concatenate(
            [
                cf[pl.ds(s * PITCH + line, blocks, stride=PITCH), :].astype(BF)
                for s in range(SHIFTS + 1)
            ],
            axis=1,
        )
        prod = lax.dot_general(
            here, later, (((0,), (0,)), ((), ())), preferred_element_type=F32
        )
        for s in range(SHIFTS):
            part = jnp.where(
                across,
                prod[:, s * LANES : (s + 1) * LANES],
                prod[:, (s + 1) * LANES : (s + 2) * LANES],
            )
            part = pltpu.roll(part, 1, 1, stride=1, stride_axis=0)
            part = jnp.sum(part.reshape(LANES // 8, 8, LANES), axis=0)
            acc[s, pl.ds(pl.multiple_of(line * 8, 8), 8), :] = part

    def windows(line):
        for s in range(SHIFTS + 1):
            span = slice(s * LANES, (s + 1) * LANES)
            lhs[line, 0:blocks, span] = xf[
                pl.ds((SHIFTS - s) * PITCH + line, blocks, stride=PITCH), :
            ].astype(BF)
            lhs[line, blocks : 2 * blocks, span] = cjf[
                pl.ds(s * PITCH + line, blocks, stride=PITCH), :
            ].astype(BF)

    def before(step, carry):
        for u in range(8):
            lag_line(step * 8 + u)
        return carry

    lax.fori_loop(0, LINES // 8, before, 0)
    scale = 1.0 / math.sqrt(2 * blocks * LANES)
    lag = jnp.concatenate(
        [
            sum(acc[s, pl.ds(r, LINES, stride=8), :] for r in range(8))
            for s in range(SHIFTS)
        ],
        axis=1,
    )
    lx_out[...] = jnp.where(tap_mask, lag, 0.0) * scale
    lag_swap = swap(lx_out, lx_in, lx_sem)
    lag_swap.start()
    ins[4].wait()
    arrived(rq_in, rq_sem)
    asked = rq_in[...].reshape(chips, BANK_ROWS)
    first = one_hot((asked == 1.0) | (asked == 3.0))
    second = one_hot(asked >= 2.0)
    owned[...] = jnp.concatenate([first, second], axis=0).astype(BF)

    def pack_slots(values, out_ref):
        for slot in range(SLOTS):
            for s in range(SHIFTS):
                stage[pl.ds(slot * SHIFTS + s, chips, stride=STEP), :] = values[
                    slot * chips : (slot + 1) * chips, s * LANES : (s + 1) * LANES
                ]
        for i in range(chips):
            out_ref[i] = stage[i * STEP : i * STEP + ROWS, :].astype(BF)

    def unpack_slots(in_ref):
        for i in range(chips):
            stage[i * STEP : i * STEP + ROWS, :] = in_ref[i].astype(F32)
        return jnp.concatenate(
            [
                jnp.concatenate(
                    [
                        stage[pl.ds(slot * SHIFTS + s, chips, stride=STEP), :]
                        for s in range(SHIFTS)
                    ],
                    axis=1,
                )
                for slot in range(SLOTS)
            ],
            axis=0,
        ).astype(BF)

    pack_slots(jnp.dot(owned[...], bank[...], preferred_element_type=F32), fe_out)
    scatter(fe_out, fe_in, fe_sem)

    def prepare(step, carry):
        for u in range(2):
            windows(step * 2 + u)
        return carry

    lag_swap.wait_recv()
    lag = (lx_out[...] + lx_in[...]).astype(BF)
    pack_slots(jnp.dot(pick_t, lag, preferred_element_type=F32), re_out)
    scatter(re_out, re_in, re_sem)
    lax.fori_loop(0, LINES // 2, prepare, 0)


    arrived(fe_in, fe_sem)
    mine = jnp.dot(pick, unpack_slots(fe_in), preferred_element_type=F32)
    kx_out[...] = jnp.where(tap_mask, mine, 0.0).astype(BF)
    tap_swaps = []
    for part in range(2):
        at = pl.ds(part * (LINES // 2), LINES // 2)
        tap_swaps.append(swap(kx_out.at[at], kx_in.at[at], kx_sem.at[part]))
        tap_swaps[-1].start()

    def settle(part):
        tap_swaps[part].wait_recv()
        at = slice(part * (LINES // 2), (part + 1) * (LINES // 2))
        taps = kx_out[at, :].astype(F32) + kx_in[at, :].astype(F32)
        for s in range(SHIFTS):
            kf[s * LINES + at.start : s * LINES + at.stop, :] = taps[
                :, s * LANES : (s + 1) * LANES
            ]

    upper = iota((LANES, LANES), 1) >= iota((LANES, LANES), 0)

    def filter_line(line):
        bands = []
        before_it = jnp.zeros((LANES, LANES), F32)
        for s in range(SHIFTS):
            row = kf[pl.ds(s * LINES + line, 1), :]
            rolled = pltpu.roll(
                jnp.broadcast_to(row, (LANES, LANES)), 0, 1, stride=1, stride_axis=0
            )
            bands.append(jnp.where(upper, rolled, before_it).astype(BF))
            before_it = rolled
        bands.append(jnp.where(upper, 0.0, before_it).astype(BF))
        both = jnp.dot(
            lhs[line], jnp.concatenate(bands, axis=0), preferred_element_type=F32
        )
        of[pl.ds(line, blocks, stride=PITCH), :] = both[:blocks]
        gf[pl.ds(line, blocks, stride=PITCH), :] = both[blocks:]

    def filters(half):
        def step_of(step, carry):
            for u in range(16):
                filter_line(half * 16 + step * 16 + u)
            return carry

        lax.fori_loop(0, 1, step_of, 0)
        at = slice(half * 16, half * 16 + 16)
        for q in range(blocks):
            span = slice(q * LANES, (q + 1) * LANES)
            from_ = slice(q * PITCH + half * 16, q * PITCH + half * 16 + 16)
            fil[at, span] = of[from_, :].astype(BF)
            grad[at, span] = jnp.dot(
                gf[from_, :].astype(BF), turn, preferred_element_type=F32
            ).astype(BF)

    arrived(re_in, re_sem)
    total = lax.dot_general(
        owned[...], unpack_slots(re_in), (((0,), (0,)), ((), ())), preferred_element_type=F32
    )
    half_taps = TAPS // 2
    gx_out[...] = jnp.where(core == 0, total[:, half_taps:], total[:, :half_taps])
    bgrad[...] = jnp.where(core == 0, total[:, :half_taps], total[:, half_taps:])
    sum_swap = swap(gx_out, gx_in, gx_sem)
    sum_swap.start()

    settle(0)
    filters(0)
    settle(1)

    filters(1)
    sum_swap.wait_recv()
    bgrad[...] = bgrad[...] + gx_in[...]

    pltpu.make_async_copy(halo, halo, halo_sem.at[0]).wait()
    departed(rq_out, rq_sem)
    departed(fe_out, fe_sem)
    departed(re_out, re_sem)
    lag_swap.wait_send()
    for tap_swap in tap_swaps:
        tap_swap.wait_send()
    sum_swap.wait_send()


def finish(fil, grad, bgrad, fil_hbm, grad_hbm, bgrad_hbm, sem):
    outs = [
        pltpu.make_async_copy(fil, fil_hbm, sem.at[0]),
        pltpu.make_async_copy(grad, grad_hbm, sem.at[1]),
        pltpu.make_async_copy(bgrad, bgrad_hbm, sem.at[2]),
    ]
    for copy in outs:
        copy.start()
    for copy in outs:
        copy.wait()


def body(signal, cotangent, bank, lengths, kernel_ids):
    line_count, samples = signal.shape
    blocks = samples // LANES
    chips = lax.axis_size("line") // 2
    any_ = pl.BlockSpec(memory_space=pl.ANY)
    vmem = pl.BlockSpec(memory_space=pltpu.VMEM)
    message = (chips, SLOTS * SHIFTS, LANES)
    pair = pltpu.SemaphoreType.DMA((2,))
    shapes = (
        ((line_count, samples), BF),
        ((line_count, samples), BF),
        ((BANK_ROWS, TAPS // 2), F32),
    )
    results = pl.pallas_call(
        kernel,
        out_shape=tuple(pltpu.VMEM(*shape) for shape in shapes),
        in_specs=[any_] * 5,
        out_specs=(vmem,) * 3,
        scratch_shapes=[
            pltpu.VMEM((line_count, samples), BF),
            pltpu.VMEM((line_count, samples), BF),
            pltpu.VMEM((BANK_ROWS, TAPS), BF),
            pltpu.VMEM((line_count,), jnp.int32),
            pltpu.VMEM((line_count,), jnp.int32),
            pltpu.VMEM((line_count, TAPS), BF),
            pltpu.VMEM((chips, 1, LANES), F32),
            pltpu.VMEM((chips, 1, LANES), F32),
            pltpu.VMEM(message, BF),
            pltpu.VMEM(message, BF),
            pltpu.VMEM(message, BF),
            pltpu.VMEM(message, BF),
            pltpu.VMEM((line_count, TAPS), BF),
            pltpu.VMEM((line_count, TAPS), BF),
            pltpu.VMEM((line_count, TAPS), F32),
            pltpu.VMEM((line_count, TAPS), F32),
            pltpu.VMEM((BANK_ROWS, TAPS // 2), F32),
            pltpu.VMEM((BANK_ROWS, TAPS // 2), F32),
            pltpu.VMEM(((blocks + SHIFTS) * PITCH, LANES), F32),
            pltpu.VMEM(((blocks + SHIFTS) * PITCH, LANES), F32),
            pltpu.VMEM(((blocks + SHIFTS) * PITCH, LANES), F32),
            pltpu.VMEM((blocks * PITCH, LANES), F32),
            pltpu.VMEM((line_count, 2 * blocks, TAPS + LANES), BF),
            pltpu.VMEM((SHIFTS, 8 * line_count, LANES), F32),
            pltpu.VMEM((SHIFTS * line_count, LANES), F32),
            pltpu.VMEM((chips * STEP, LANES), F32),
            pltpu.VMEM((SLOTS * chips, BANK_ROWS), BF),
            pltpu.VMEM((blocks * PITCH, LANES), F32),
            pltpu.VMEM((blocks * PITCH, LANES), F32),
            pltpu.SemaphoreType.DMA((5,)),
            pair, pair, pair, pair, pltpu.SemaphoreType.DMA((2, 2)), pair, pair,
        ],
        compiler_params=pltpu.CompilerParams(
            collective_id=0, has_side_effects=True, vmem_limit_bytes=60 * 1024 * 1024
        ),
        cost_estimate=pl.CostEstimate(
            flops=6 * line_count * samples * TAPS, bytes_accessed=1 << 21, transcendentals=0
        ),
    )(signal, cotangent, bank, lengths, kernel_ids)
    return pl.pallas_call(
        finish,
        out_shape=tuple(jax.ShapeDtypeStruct(*shape) for shape in shapes),
        in_specs=[vmem] * 3,
        out_specs=(any_,) * 3,
        scratch_shapes=[pltpu.SemaphoreType.DMA((3,))],
    )(*[pltpu.with_memory_space_constraint(r, pltpu.VMEM) for r in results])


def solution(mesh):
    return jax.shard_map(
        body,
        mesh=mesh,
        in_specs=(P("line", "tm"), P("line", "tm"), P("line", None), P("line"), P("line")),
        out_specs=(P("line", "tm"), P("line", "tm"), P("line", "tm")),
        check_vma=False,
    )
```
